32 devices in a mesh: dp: 4 (over z), tensor: 8 (over y, x, core).
Axes of the slice: x: 2, y: 2, z: 4, core: 2. Of those that a mesh axis runs over, the one named last changes fastest.
Arguments:
- inputs: bfloat16 [4096, 8192], P('dp', 'tensor'), may hold values from -6 to 6
- output_gradient: bfloat16 [4096, 8192], P('dp', 'tensor'), may hold values from -6 to 6
- weight: bfloat16 [8192, 8192], P(None, 'tensor'), may hold values from -0.0625 to 0.0625
- adapter_down_factor: bfloat16 [512, 16, 8192], P('dp', None, 'tensor'), may hold values from -0.0625 to 0.0625
- adapter_up_factor: bfloat16 [512, 16, 8192], P('dp', None, 'tensor'), may hold values from -0.0625 to 0.0625
- block_adapter_index: int32 [32], P('dp'), may hold values from 0 to 511
- adapter_table_slot: int32 [512], replicated, may hold values from 0 to 511, each once
Outputs:
- input_gradient: bfloat16 [4096, 8192], P('dp', 'tensor')
- grad_down: float32 [512, 16, 8192], P('dp', None, 'tensor')
- grad_up: float32 [512, 16, 8192], P('dp', None, 'tensor')
The draws below stay inside these ranges and needn't reach their ends.
Inputs may be any that keep to these rules, and one draw needn't show every extreme that they name: `adapter_table_slot`: each slot is used by exactly one adapter.
All inputs are finite; a program needn't handle non-finite values.
Results may differ from the reference program's by a relative error of at most 0.003.
Values may be sent and summed in bfloat16 or wider, within the bound.
A program may use at most 192 MiB of HBM per device.

```python
import math
import jax
import jax.numpy as jnp
import numpy as np

MODEL_WIDTH = 8192
ADAPTER_RANK = 16
BLOCK = 128
ADAPTER_TOTAL = 512
TOKEN_ROWS = 4096
BLOCKS = 32


def place_ends(drawn, key, least, high):
    spot = [jax.random.randint(jax.random.fold_in(key, axis), (), 0, length) for axis, length in enumerate(drawn.shape)]
    main_axis = drawn.shape.index(max(drawn.shape))
    neighbour = spot[:main_axis] + [(spot[main_axis] + 1) % drawn.shape[main_axis]] + spot[main_axis + 1:]
    return drawn.at[tuple(spot)].set(least).at[tuple(neighbour)].set(high)


def block_levels(stream_key, shape, split, low, high):
    def one(position, parts):
        steps = jax.random.uniform(jax.random.fold_in(jax.random.fold_in(stream_key, 6), position), (parts,), jnp.float32, low / len(split), high / len(split))
        return jnp.repeat(jnp.exp(steps), shape[position] // parts).reshape((-1,) + (1,) * (len(shape) - position - 1))

    level = one(*split[0])
    for cut in split[1:]:
        level = level * one(*cut)
    return level


def rank_bounds(amount, skew):
    loads = [(1 << 20) // math.isqrt(standing ** skew) + 1 for standing in range(1, amount + 1)]
    scale = 1 + sum(loads) // (1 << 30)
    return np.cumsum(np.array([max(1, weight // scale) for weight in loads]))


def ranked(stream_key, extent, count, slope):
    table = rank_bounds(count, slope)
    ticket = jax.random.randint(jax.random.fold_in(stream_key, 1), extent, 0, int(table[count - 1]))
    standing = jnp.searchsorted(jnp.asarray(table, jnp.int32), ticket, side="right")
    return jax.random.permutation(jax.random.fold_in(stream_key, 2), count)[standing].astype(jnp.int32)


def scatter_about(rng, dims, deviation, most, cuts=(), held_as=jnp.bfloat16):
    result = deviation * jax.random.normal(rng, dims, jnp.float32)
    if cuts:
        result = result * block_levels(rng, dims, cuts, -0.22, 0.18)
    return jnp.clip(result, -most, most).astype(held_as)


def setup_inputs(seed: int = 0) -> dict:
    arg_keys = jax.random.split(jax.random.key(seed), 8)
    inputs = scatter_about(arg_keys[0], (TOKEN_ROWS, MODEL_WIDTH), 1.0, 6.0, ((0, 4), (1, 8)))
    output_gradient = scatter_about(arg_keys[1], (TOKEN_ROWS, MODEL_WIDTH), 1.0, 6.0, ((0, 4), (1, 8)))
    weight = scatter_about(arg_keys[2], (MODEL_WIDTH, MODEL_WIDTH), MODEL_WIDTH ** -0.5, 0.0625, ((1, 8),))
    adapter_down_factor = scatter_about(arg_keys[3], (ADAPTER_TOTAL, ADAPTER_RANK, MODEL_WIDTH), MODEL_WIDTH ** -0.5, 0.0625, ((0, 4), (2, 8)))
    adapter_up_factor = scatter_about(arg_keys[4], (ADAPTER_TOTAL, ADAPTER_RANK, MODEL_WIDTH), MODEL_WIDTH ** -0.5, 0.0625, ((0, 4), (2, 8)))
    block_adapter_index = place_ends(ranked(arg_keys[5], (BLOCKS,), ADAPTER_TOTAL, 2), jax.random.fold_in(arg_keys[5], 3), 0, ADAPTER_TOTAL - 1).astype(jnp.int32)
    adapter_table_slot = jax.random.permutation(arg_keys[6], ADAPTER_TOTAL).astype(jnp.int32)
    return dict(inputs=inputs, output_gradient=output_gradient, weight=weight, adapter_down_factor=adapter_down_factor, adapter_up_factor=adapter_up_factor, block_adapter_index=block_adapter_index, adapter_table_slot=adapter_table_slot)


adapter_scale = 2.0


def reference(inputs, output_gradient, weight, adapter_down_factor, adapter_up_factor, block_adapter_index, adapter_table_slot):
    slot_index_list = adapter_table_slot[block_adapter_index].astype(jnp.int32)
    down_factor_blocks = adapter_down_factor[slot_index_list].astype(jnp.float32)
    up_factor_blocks = adapter_up_factor[slot_index_list].astype(jnp.float32)
    input_blocks = inputs.reshape(BLOCKS, BLOCK, MODEL_WIDTH).astype(jnp.float32)
    output_gradient_blocks = output_gradient.reshape(BLOCKS, BLOCK, MODEL_WIDTH).astype(jnp.float32)
    hidden_activation = jnp.einsum("nvh,nwh->nvw", input_blocks, down_factor_blocks)
    projected_gradient = jnp.einsum("nvh,nwh->nvw", output_gradient_blocks, up_factor_blocks)
    hidden_lowrank = hidden_activation.astype(jnp.bfloat16).astype(jnp.float32)
    projected_gradient_lowrank = projected_gradient.astype(jnp.bfloat16).astype(jnp.float32)
    frozen_input_gradient = jnp.dot(output_gradient, weight.T, preferred_element_type=jnp.float32)
    adapter_input_gradient = jnp.einsum("wmx,wxv->wmv", projected_gradient_lowrank, down_factor_blocks).reshape(TOKEN_ROWS, MODEL_WIDTH)
    input_gradient = (frozen_input_gradient + adapter_scale * adapter_input_gradient).astype(jnp.bfloat16)
    block_down_factor = adapter_scale * jnp.einsum("eyw,eyi->ewi", projected_gradient_lowrank, input_blocks)
    block_up_factor = adapter_scale * jnp.einsum("eyw,eyi->ewi", hidden_lowrank, output_gradient_blocks)
    grad_down = jnp.zeros((ADAPTER_TOTAL, ADAPTER_RANK, MODEL_WIDTH), jnp.float32).at[slot_index_list].add(block_down_factor)
    grad_up = jnp.zeros((ADAPTER_TOTAL, ADAPTER_RANK, MODEL_WIDTH), jnp.float32).at[slot_index_list].add(block_up_factor)
    return input_gradient, grad_down, grad_up
```

```python
import jax
import jax.numpy as jnp
from jax import lax
from jax.experimental import pallas as pl
from jax.experimental.pallas import tpu as pltpu
from jax.sharding import PartitionSpec as P

BLOCK = 128

adapter_scale = 2.0


def scatter_kernel(slots_ref, arrived_ref, down_ref, up_ref):
    chunk, rank = down_ref.shape[0], down_ref.shape[1]
    first = pl.program_id(0) * chunk
    down_ref[...] = jnp.zeros_like(down_ref)
    up_ref[...] = jnp.zeros_like(up_ref)

    @pl.loop(0, arrived_ref.shape[0])
    def _(b):
        row = slots_ref[b] - first

        @pl.when((row >= 0) & (row < chunk))
        def _():
            down_ref[row] += arrived_ref[b, :rank].astype(jnp.float32)
            up_ref[row] += arrived_ref[b, rank:].astype(jnp.float32)


def scatter_by_slot(local_slots, arrived, owned, rank, width):
    chunk = 16
    out = jax.ShapeDtypeStruct((owned, rank, width), jnp.float32)
    out_spec = pl.BlockSpec((chunk, rank, width), lambda i, s: (i, 0, 0))
    return pl.pallas_call(
        scatter_kernel,
        out_shape=(out, out),
        grid_spec=pltpu.PrefetchScalarGridSpec(
            num_scalar_prefetch=1,
            grid=(owned // chunk,),
            in_specs=[pl.BlockSpec(arrived.shape, lambda i, s: (0, 0, 0))],
            out_specs=(out_spec, out_spec),
        ),
        compiler_params=pltpu.CompilerParams(vmem_limit_bytes=24 * 2**20),
        cost_estimate=pl.CostEstimate(
            flops=0, bytes_accessed=2 * owned * rank * width * 4, transcendentals=0
        ),
    )(local_slots, arrived)


def pick_kernel(slots_ref, down_ref, up_ref, out_ref, held, sem):
    owned, rank = down_ref.shape[0], down_ref.shape[1]
    count = out_ref.shape[0]

    def copies(b):
        slot = slots_ref[b]
        slot = jnp.where((slot >= 0) & (slot < owned), slot, 0)
        return [
            pltpu.make_async_copy(ref.at[slot], held.at[b, i], sem.at[b, i])
            for i, ref in enumerate((down_ref, up_ref))
        ]

    @pl.loop(0, count)
    def _(b):
        for copy in copies(b):
            copy.start()

    @pl.loop(0, count)
    def _(b):
        for copy in copies(b):
            copy.wait()
        mine = (slots_ref[b] >= 0) & (slots_ref[b] < owned)

        @pl.when(mine)
        def _():
            out_ref[b, :rank] = held[b, 0]
            out_ref[b, rank:] = held[b, 1]

        @pl.when(jnp.logical_not(mine))
        def _():
            out_ref[b] = jnp.zeros(out_ref.shape[1:], out_ref.dtype)


def pick_by_slot(local_slots, down, up):
    count = local_slots.shape[0]
    rank, width = down.shape[1:]
    return pl.pallas_call(
        pick_kernel,
        out_shape=jax.ShapeDtypeStruct((count, 2 * rank, width), down.dtype),
        grid_spec=pltpu.PrefetchScalarGridSpec(
            num_scalar_prefetch=1,
            grid=(1,),
            in_specs=[pl.BlockSpec(memory_space=pl.ANY)] * 2,
            out_specs=pl.BlockSpec((count, 2 * rank, width), lambda i, s: (0, 0, 0)),
            scratch_shapes=[
                pltpu.VMEM((count, 2, rank, width), down.dtype),
                pltpu.SemaphoreType.DMA((count, 2)),
            ],
        ),
        compiler_params=pltpu.CompilerParams(vmem_limit_bytes=24 * 2**20),
        cost_estimate=pl.CostEstimate(
            flops=0, bytes_accessed=4 * count * rank * width * 4, transcendentals=0
        ),
    )(local_slots, down, up)


def base_terms(output_gradient, weight, n):
    rows, width = output_gradient.shape
    t = lax.axis_index("tensor")
    dims = (((1,), (1,)), ((), ()))

    def dot(a, w):
        return lax.dot_general(a, w, dims, preferred_element_type=jnp.float32)

    if n != 8:
        whole = dot(output_gradient, weight)
        return [lax.psum_scatter(whole, "tensor", scatter_dimension=1, tiled=True)]

    def swap(value, bit):
        return lax.ppermute(value, "tensor", [(i, i ^ bit) for i in range(n)])

    def rows_of(owner):
        return lax.dynamic_slice_in_dim(weight, owner * width, width, 0)

    def low(value):
        return value.astype(jnp.bfloat16)

    sibling_gradient = swap(output_gradient, 1)
    sibling_rows = {k: swap(rows_of(t ^ (2 * k) ^ 1), 1) for k in (3, 1, 2, 0)}
    own = {k: dot(output_gradient, rows_of(t ^ (2 * k))) for k in (3, 1, 2, 0)}
    chip_sum = {k: own[k] + dot(sibling_gradient, sibling_rows[k]) for k in (3, 1, 2, 0)}
    h = rows // 2
    diag_a = swap(low(chip_sum[3][:h]), 2)
    diag_b = swap(low(chip_sum[3][h:]), 4)
    x_a = swap(low(chip_sum[1][:h]), 2)
    y_b = swap(low(chip_sum[2][h:]), 4)
    y_a = swap(low(chip_sum[2][:h] + diag_a.astype(jnp.float32)), 4)
    x_b = swap(low(chip_sum[1][h:] + diag_b.astype(jnp.float32)), 2)
    return [
        chip_sum[0],
        jnp.concatenate((x_a, x_b), axis=0).astype(jnp.float32),
        jnp.concatenate((y_a, y_b), axis=0).astype(jnp.float32),
    ]


def per_device(
    inputs,
    output_gradient,
    weight,
    adapter_down_factor,
    adapter_up_factor,
    block_adapter_index,
    adapter_table_slot,
):
    row_count = inputs.shape[0]
    block_count = row_count // BLOCK
    rank = adapter_down_factor.shape[1]
    width = inputs.shape[1]
    owned = adapter_down_factor.shape[0]
    owner_id = lax.axis_index("dp")
    n = lax.axis_size("tensor")

    table_ids = lax.broadcasted_iota(jnp.int32, (block_count, adapter_table_slot.shape[0]), 1)
    my_slots = jnp.sum(
        jnp.where(block_adapter_index[:, None] == table_ids, adapter_table_slot[None, :], 0), axis=1
    )
    all_slots = lax.all_gather(my_slots, "dp", axis=0, tiled=True)
    local_slots = all_slots - owner_id * owned

    terms = base_terms(output_gradient, weight, n)

    fetched = lax.psum_scatter(
        pick_by_slot(local_slots, adapter_down_factor, adapter_up_factor),
        "dp",
        scatter_dimension=0,
        tiled=True,
    )
    down, up = fetched[:, :rank], fetched[:, rank:]
    input_blocks = inputs.reshape(block_count, BLOCK, width)
    gradient_blocks = output_gradient.reshape(block_count, BLOCK, width)
    hidden_part = jnp.einsum("nvh,nwh->nwv", input_blocks, down, preferred_element_type=jnp.float32)
    gproj_part = jnp.einsum("nvh,nwh->nwv", gradient_blocks, up, preferred_element_type=jnp.float32)
    both = lax.psum(jnp.concatenate((gproj_part, hidden_part), axis=1), "tensor")
    both = both.astype(jnp.bfloat16)
    gproj, hidden = both[:, :rank], both[:, rank:]
    block_down = adapter_scale * jnp.einsum(
        "nwv,nvh->nwh", gproj, input_blocks, preferred_element_type=jnp.float32
    )
    block_up = adapter_scale * jnp.einsum(
        "nwv,nvh->nwh", hidden, gradient_blocks, preferred_element_type=jnp.float32
    )
    block_grads = jnp.concatenate((block_down, block_up), axis=1).astype(jnp.bfloat16)
    arrived = lax.all_gather(block_grads, "dp", axis=0, tiled=True)
    grad_down, grad_up = scatter_by_slot(local_slots, arrived, owned, rank, width)

    adapter_part = jnp.einsum(
        "nwv,nwh->nvh", gproj, down, preferred_element_type=jnp.float32
    ).reshape(row_count, width)
    total = adapter_scale * adapter_part
    for term in terms:
        total = total + term
    return total.astype(jnp.bfloat16), grad_down, grad_up


def solution(mesh):
    return jax.shard_map(
        per_device,
        mesh=mesh,
        in_specs=(
            P("dp", "tensor"),
            P("dp", "tensor"),
            P(None, "tensor"),
            P("dp", None, "tensor"),
            P("dp", None, "tensor"),
            P("dp"),
            P(),
        ),
        out_specs=(P("dp", "tensor"), P("dp", None, "tensor"), P("dp", None, "tensor")),
        check_vma=False,
    )
```

```python
import jax
import jax.numpy as jnp
from jax import lax
from jax.experimental import pallas as pl
from jax.experimental.pallas import tpu as pltpu
from jax.sharding import PartitionSpec as P

BLOCK = 128

adapter_scale = 2.0


def scatter_kernel(slots_ref, arrived_down, arrived_up, down_ref, up_ref):
    chunk = down_ref.shape[0]
    first = pl.program_id(0) * chunk
    down_ref[...] = jnp.zeros_like(down_ref)
    up_ref[...] = jnp.zeros_like(up_ref)

    @pl.loop(0, arrived_down.shape[0])
    def _(b):
        row = slots_ref[b] - first

        @pl.when((row >= 0) & (row < chunk))
        def _():
            down_ref[row] += arrived_down[b].astype(jnp.float32)
            up_ref[row] += arrived_up[b].astype(jnp.float32)


def scatter_by_slot(local_slots, arrived_down, arrived_up, owned):
    rank, width = arrived_down.shape[1:]
    chunk = 16
    out = jax.ShapeDtypeStruct((owned, rank, width), jnp.float32)
    out_spec = pl.BlockSpec((chunk, rank, width), lambda i, s: (i, 0, 0))
    return pl.pallas_call(
        scatter_kernel,
        out_shape=(out, out),
        grid_spec=pltpu.PrefetchScalarGridSpec(
            num_scalar_prefetch=1,
            grid=(owned // chunk,),
            in_specs=[pl.BlockSpec(arrived_down.shape, lambda i, s: (0, 0, 0))] * 2,
            out_specs=(out_spec, out_spec),
        ),
        compiler_params=pltpu.CompilerParams(vmem_limit_bytes=56 * 2**20),
        cost_estimate=pl.CostEstimate(
            flops=0, bytes_accessed=2 * owned * rank * width * 4, transcendentals=0
        ),
    )(local_slots, arrived_down, arrived_up)


def pick_kernel(slots_ref, down_ref, up_ref, down_out, up_out, held, sem):
    owned = down_ref.shape[0]
    count = down_out.shape[0]

    def copies(b):
        slot = slots_ref[b]
        slot = jnp.where((slot >= 0) & (slot < owned), slot, 0)
        return [
            pltpu.make_async_copy(ref.at[slot], held.at[b, i], sem.at[b, i])
            for i, ref in enumerate((down_ref, up_ref))
        ]

    @pl.loop(0, count)
    def _(b):
        for copy in copies(b):
            copy.start()

    @pl.loop(0, count)
    def _(b):
        for copy in copies(b):
            copy.wait()
        mine = (slots_ref[b] >= 0) & (slots_ref[b] < owned)

        @pl.when(mine)
        def _():
            down_out[b] = held[b, 0]
            up_out[b] = held[b, 1]

        @pl.when(jnp.logical_not(mine))
        def _():
            down_out[b] = jnp.zeros(down_out.shape[1:], down_out.dtype)
            up_out[b] = jnp.zeros(up_out.shape[1:], up_out.dtype)


def pick_by_slot(local_slots, down, up):
    count = local_slots.shape[0]
    rank, width = down.shape[1:]
    out = jax.ShapeDtypeStruct((count, rank, width), down.dtype)
    out_spec = pl.BlockSpec((count, rank, width), lambda i, s: (0, 0, 0))
    return pl.pallas_call(
        pick_kernel,
        out_shape=(out, out),
        grid_spec=pltpu.PrefetchScalarGridSpec(
            num_scalar_prefetch=1,
            grid=(1,),
            in_specs=[pl.BlockSpec(memory_space=pltpu.HBM)] * 2,
            out_specs=(out_spec, out_spec),
            scratch_shapes=[
                pltpu.VMEM((count, 2, rank, width), down.dtype),
                pltpu.SemaphoreType.DMA((count, 2)),
            ],
        ),
        compiler_params=pltpu.CompilerParams(vmem_limit_bytes=56 * 2**20),
        cost_estimate=pl.CostEstimate(
            flops=0, bytes_accessed=4 * count * rank * width * 4, transcendentals=0
        ),
    )(local_slots, down, up)


def chip_sum_kernel(owner_ref, g_ref, other_g_ref, w_ref, other_w_ref, first_ref, second_ref):
    dims = (((1,), (1,)), ((), ()))
    total = lax.dot_general(g_ref[...], w_ref[...], dims, preferred_element_type=jnp.float32)
    total += lax.dot_general(
        other_g_ref[...], other_w_ref[...], dims, preferred_element_type=jnp.float32
    )
    h = first_ref.shape[0]
    first_ref[...] = total[:h].astype(first_ref.dtype)
    second_ref[...] = total[h:].astype(second_ref.dtype)


def chip_sum(owner, gradient, other_gradient, weight, other_rows, first, second):
    rows, depth = gradient.shape
    width = other_rows.shape[0]
    tile = 256
    h = rows // 2
    whole = pl.BlockSpec((rows, depth), lambda j, o: (0, 0))
    out = pl.BlockSpec((h, tile), lambda j, o: (0, j))
    return pl.pallas_call(
        chip_sum_kernel,
        out_shape=(
            jax.ShapeDtypeStruct((h, width), first),
            jax.ShapeDtypeStruct((h, width), second),
        ),
        grid_spec=pltpu.PrefetchScalarGridSpec(
            num_scalar_prefetch=1,
            grid=(width // tile,),
            in_specs=[
                whole,
                whole,
                pl.BlockSpec((tile, depth), lambda j, o: (o[0] * (width // tile) + j, 0)),
                pl.BlockSpec((tile, depth), lambda j, o: (j, 0)),
            ],
            out_specs=(out, out),
        ),
        compiler_params=pltpu.CompilerParams(vmem_limit_bytes=56 * 2**20),
        cost_estimate=pl.CostEstimate(
            flops=4 * rows * depth * width, bytes_accessed=12 * 2**20, transcendentals=0
        ),
    )(owner.reshape(1), gradient, other_gradient, weight, other_rows)


def final_kernel(own_a, own_b, x_a, x_b, y_a, y_b, gproj_ref, down_ref, out_ref):
    for half, (own, x, y) in enumerate(((own_a, x_a, y_a), (own_b, x_b, y_b))):
        adapter = lax.dot_general(
            gproj_ref[half, 0],
            down_ref[half, 0],
            (((0,), (0,)), ((), ())),
            preferred_element_type=jnp.float32,
        )
        total = own[...] + x[...].astype(jnp.float32) + y[...].astype(jnp.float32)
        out_ref[half] = (total + adapter_scale * adapter).astype(out_ref.dtype)


def final_sum(pieces, gproj, down):
    h, width = pieces[0].shape
    rank = gproj.shape[1]
    pairs = h // BLOCK
    piece = pl.BlockSpec((BLOCK, width), lambda i: (i, 0))
    return pl.pallas_call(
        final_kernel,
        out_shape=jax.ShapeDtypeStruct((2, h, width), jnp.bfloat16),
        grid=(pairs,),
        in_specs=[piece] * 6
        + [
            pl.BlockSpec((2, 1, rank, BLOCK), lambda i: (0, i, 0, 0)),
            pl.BlockSpec((2, 1, rank, width), lambda i: (0, i, 0, 0)),
        ],
        out_specs=pl.BlockSpec((2, BLOCK, width), lambda i: (0, i, 0)),
        compiler_params=pltpu.CompilerParams(vmem_limit_bytes=56 * 2**20),
        cost_estimate=pl.CostEstimate(flops=0, bytes_accessed=10 * 2**20, transcendentals=0),
    )(
        *pieces,
        gproj.reshape(2, pairs, rank, BLOCK),
        down.reshape(2, pairs, rank, width),
    ).reshape(2 * h, width)


def swap(value, bit):
    n = lax.axis_size("tensor")
    return lax.ppermute(value, "tensor", [(i, i ^ bit) for i in range(n)])


def sum_over_tensor(value):
    if lax.axis_size("tensor") != 8:
        return lax.psum(value, "tensor")
    for bit in (1, 2, 4):
        value = value + swap(value, bit)
    return value


def sibling_slice(weight, width, k):
    t = lax.axis_index("tensor")
    return lax.dynamic_slice_in_dim(weight, (t ^ (2 * k) ^ 1) * width, width, 0)


def base_pieces(output_gradient, sibling_gradient, weight, diagonal_rows):
    width = output_gradient.shape[1]
    t = lax.axis_index("tensor")
    low, high = jnp.bfloat16, jnp.float32
    sibling_rows = {3: diagonal_rows}
    for k in (1, 2, 0):
        sibling_rows[k] = swap(sibling_slice(weight, width, k), 1)

    def both(k, first, second):
        return chip_sum(
            t ^ (2 * k), output_gradient, sibling_gradient, weight, sibling_rows[k], first, second
        )

    diag_first, diag_second = both(3, low, low)
    diag_a, diag_b = swap(diag_first, 2), swap(diag_second, 4)
    x_first, x_second = both(1, low, high)
    y_first, y_second = both(2, high, low)
    y_through = (y_first + diag_a.astype(high)).astype(low)
    x_through = (x_second + diag_b.astype(high)).astype(low)
    own_first, own_second = both(0, high, high)
    pieces = swap(x_first, 2), swap(x_through, 2), swap(y_through, 4), swap(y_second, 4)
    early = x_through, y_through, own_first, pieces[0], pieces[3]
    return (own_first, own_second, *pieces), early


def per_device(
    inputs,
    output_gradient,
    weight,
    adapter_down_factor,
    adapter_up_factor,
    block_adapter_index,
    adapter_table_slot,
):
    row_count = inputs.shape[0]
    block_count = row_count // BLOCK
    rank = adapter_down_factor.shape[1]
    width = inputs.shape[1]
    owned = adapter_down_factor.shape[0]
    owner_id = lax.axis_index("dp")
    n = lax.axis_size("tensor")

    if n == 8:
        diagonal_rows, block_adapter_index = lax.optimization_barrier(
            (sibling_slice(weight, width, 3), block_adapter_index)
        )
    table_ids = lax.broadcasted_iota(jnp.int32, (block_count, adapter_table_slot.shape[0]), 1)
    my_slots = jnp.sum(
        jnp.where(block_adapter_index[:, None] == table_ids, adapter_table_slot[None, :], 0), axis=1
    )
    all_slots = lax.all_gather(my_slots, "dp", axis=0, tiled=True)
    local_slots = all_slots - owner_id * owned

    if n == 8:
        sibling_gradient, diagonal_rows, local_slots = lax.optimization_barrier(
            (swap(output_gradient, 1), swap(diagonal_rows, 1), local_slots)
        )
    down_picked, up_picked = pick_by_slot(local_slots, adapter_down_factor, adapter_up_factor)
    up = lax.psum_scatter(up_picked, "dp", scatter_dimension=0, tiled=True)
    down = lax.psum_scatter(down_picked, "dp", scatter_dimension=0, tiled=True)
    if n == 8:
        pieces, sums = base_pieces(output_gradient, sibling_gradient, weight, diagonal_rows)
        up, down, _ = lax.optimization_barrier((up, down, sums))
    input_blocks = inputs.reshape(block_count, BLOCK, width)
    gradient_blocks = output_gradient.reshape(block_count, BLOCK, width)

    def project(blocks, factor):
        part = jnp.einsum("nvh,nwh->nwv", blocks, factor, preferred_element_type=jnp.float32)
        return sum_over_tensor(part).astype(jnp.bfloat16)

    def gathered(low_rank, blocks):
        grads = adapter_scale * jnp.einsum(
            "nwv,nvh->nwh", low_rank, blocks, preferred_element_type=jnp.float32
        )
        return lax.all_gather(grads.astype(jnp.bfloat16), "dp", axis=0, tiled=True)

    gproj = project(gradient_blocks, up)
    arrived_down = gathered(gproj, input_blocks)
    hidden = project(input_blocks, down)
    arrived_up = gathered(hidden, gradient_blocks)
    grad_down, grad_up = scatter_by_slot(local_slots, arrived_down, arrived_up, owned)
    if n == 8:
        return final_sum(pieces, gproj, down), grad_down, grad_up

    frozen = lax.psum_scatter(
        lax.dot_general(
            output_gradient, weight, (((1,), (1,)), ((), ())), preferred_element_type=jnp.float32
        ),
        "tensor",
        scatter_dimension=1,
        tiled=True,
    )
    adapter_part = jnp.einsum(
        "nwv,nwh->nvh", gproj, down, preferred_element_type=jnp.float32
    ).reshape(row_count, width)
    total = frozen + adapter_scale * adapter_part
    return total.astype(jnp.bfloat16), grad_down, grad_up


def solution(mesh):
    return jax.shard_map(
        per_device,
        mesh=mesh,
        in_specs=(
            P("dp", "tensor"),
            P("dp", "tensor"),
            P(None, "tensor"),
            P("dp", None, "tensor"),
            P("dp", None, "tensor"),
            P("dp"),
            P(),
        ),
        out_specs=(P("dp", "tensor"), P("dp", None, "tensor"), P("dp", None, "tensor")),
        check_vma=False,
    )
```
